1024 devices in a mesh: blk: 32 (over y, z_lo), dp: 32 (over z_hi, x, core).
Axes of the slice: x: 4, y: 4, z: 32 (z_hi: 4, z_lo: 8; z = z_hi * 8 + z_lo), core: 2. Of those that a mesh axis runs over, the one named last changes fastest.
Arguments:
- image_emb: bfloat16 [16384, 1024], P(('blk', 'dp')), may hold values from -2 to 2
- text_emb: bfloat16 [16384, 1024], P(('blk', 'dp')), may hold values from -2 to 2
Outputs:
- grad_image: float32 [16384, 1024], P(('blk', 'dp'))
- grad_text: float32 [16384, 1024], P(('blk', 'dp'))
- row_loss: float32 [16384], P(('blk', 'dp'))
The draws below stay inside these ranges and needn't reach their ends.
All inputs are finite; a program needn't handle non-finite values.
Results may differ from the reference program's by a relative error of at most 0.0029.
Values may be sent and summed in bfloat16 or wider, within the bound.
No kernel may reach another device: no remote copies, remote signals or barrier semaphores. Data moves between devices by JAX's collectives and lax.ppermute only.
A program may use at most 32 MiB of HBM per device.

```python
import math
import jax
import jax.numpy as jnp
from jax import lax

E = 1024
BATCH = 16384
GRP = 512


def pair_fields(key, scale_lo, scale_hi):
    keys = jax.random.split(key, 6)
    base = 0.3 / math.sqrt(E)
    images = jax.random.normal(keys[0], (BATCH, E), jnp.float32)
    texts = jax.random.normal(keys[1], (BATCH, E), jnp.float32)
    trend = 1.0 + 2.0 * jnp.arange(BATCH, dtype=jnp.float32) / BATCH
    lower = math.log(scale_lo)
    upper = math.log(scale_hi)
    image_scale = jnp.exp(jax.random.uniform(keys[3], (BATCH, 1), jnp.float32, lower, upper)) * trend[:, None]
    text_scale = jnp.exp(jax.random.uniform(keys[4], (BATCH, 1), jnp.float32, lower, upper)) * trend[:, None]
    images = images * image_scale * base
    texts = texts * text_scale * base
    noise = jax.random.normal(keys[5], (4, E), jnp.float32) * (0.1 * base)
    strengths = [2.2, 2.6, 3.0, 3.4]
    for which in range(4):
        target = (2 * which + 1) * BATCH // 8
        source = (target + BATCH // 2 + 3) % BATCH
        partner = (source + 1) % BATCH
        vector = texts[source]
        length = jnp.sum(vector * vector)
        images = images.at[target].set(strengths[which] * vector / length)
        texts = texts.at[partner].set(vector * (1.0 - 0.02 / strengths[which]) + noise[which])
    return (jnp.clip(images, -2.0, 2.0), jnp.clip(texts, -2.0, 2.0))


def draw_image_emb(key, part):
    images, texts = pair_fields(key, 0.5, 2.0)
    return images.astype(jnp.bfloat16)


def draw_text_emb(key, part):
    images, texts = pair_fields(key, 0.5, 2.0)
    return texts.astype(jnp.bfloat16)


def setup_inputs(seed: int = 0) -> dict:
    key_list = jax.random.split(jax.random.key(seed), 3)
    image_emb = draw_image_emb(jax.random.fold_in(key_list[2], 71), 0)
    text_emb = draw_text_emb(jax.random.fold_in(key_list[2], 71), 0)
    return {"image_emb": image_emb, "text_emb": text_emb}


logit_scale = 100.0


def reference(image_emb, text_emb):
    blocks = BATCH // GRP
    image_blocks = image_emb.reshape(blocks, GRP, E)

    def first(carry, block):
        col_max, col_sum = carry
        scores = logit_scale * jnp.dot(block, text_emb.T, preferred_element_type=jnp.float32)
        row_max = jnp.max(scores, axis=1)
        row_lse = row_max + jnp.log(jnp.sum(jnp.exp(scores - row_max[:, None]), axis=1))
        new_max = jnp.maximum(col_max, jnp.max(scores, axis=0))
        col_sum = col_sum * jnp.exp(col_max - new_max) + jnp.sum(jnp.exp(scores - new_max[None, :]), axis=0)
        return (new_max, col_sum), row_lse

    start = (jnp.full((BATCH,), -jnp.inf, jnp.float32), jnp.zeros((BATCH,), jnp.float32))
    (col_max, col_sum), row_parts = lax.scan(first, start, image_blocks)
    col_lse = col_max + jnp.log(col_sum)
    row_lse = row_parts.reshape(BATCH)

    def second(total, parts):
        block, lse_rows = parts
        scores = logit_scale * jnp.dot(block, text_emb.T, preferred_element_type=jnp.float32)
        weights = (0.5 * (jnp.exp(scores - lse_rows[:, None]) + jnp.exp(scores - col_lse[None, :]))).astype(jnp.bfloat16)
        image_part = jnp.dot(weights, text_emb, preferred_element_type=jnp.float32)
        total = total + lax.dot_general(weights, block, (((0,), (0,)), ((), ())), preferred_element_type=jnp.float32)
        return total, image_part

    text_total, image_parts = lax.scan(second, jnp.zeros((BATCH, E), jnp.float32), (image_blocks, row_parts))
    grad_image = logit_scale * image_parts.reshape(BATCH, E) - logit_scale * text_emb.astype(jnp.float32)
    grad_text = logit_scale * text_total - logit_scale * image_emb.astype(jnp.float32)
    diag = logit_scale * jnp.sum(image_emb.astype(jnp.float32) * text_emb.astype(jnp.float32), axis=1)
    row_loss = 0.5 * (row_lse + col_lse) - diag
    return grad_image, grad_text, row_loss
```

```python
import jax
import jax.numpy as jnp
from jax import lax
from jax.sharding import Mesh, PartitionSpec as P

logit_scale = 100.0

fine = {"y": 4, "zl": 8, "zh": 4, "x": 4, "core": 2}
chip = ("x", "core")
dp = ("zh", "x", "core")
blk = ("y", "zl")
everything = ("y", "zl", "zh", "x", "core")


def gather(rows, axis):
    copies = jnp.broadcast_to(rows[None], (lax.axis_size(axis),) + rows.shape)
    return lax.all_to_all(copies, axis, 0, 0)


def lse_all(scores, dim, axis):
    top = jnp.max(scores, axis=dim, keepdims=True)
    own = jnp.squeeze(top, dim) + jnp.log(jnp.sum(jnp.exp(scores - top), axis=dim))
    every = gather(own, axis)
    top = jnp.max(every, axis=0)
    return top + jnp.log(jnp.sum(jnp.exp(every - top[None]), axis=0))


def scatter_sum(parts, axis):
    return jnp.sum(
        lax.all_to_all(parts.astype(jnp.bfloat16), axis, 0, 0).astype(jnp.float32), axis=0
    )


def body(image_emb, text_emb):
    own_rows, width = image_emb.shape
    img_rows = gather(gather(image_emb, "zh"), chip).reshape(-1, width)
    txt_cols = gather(gather(text_emb, "zl"), "y").reshape(-1, width)
    scores = logit_scale * jnp.dot(img_rows, txt_cols.T, preferred_element_type=jnp.float32)
    row_lse = lse_all(scores, 1, dp)
    col_lse = lse_all(scores, 0, blk)
    weights = (
        0.5 * (jnp.exp(scores - row_lse[:, None]) + jnp.exp(scores - col_lse[None, :]))
    ).astype(jnp.bfloat16)
    image_part = jnp.dot(weights, txt_cols, preferred_element_type=jnp.float32)
    image_part = image_part.reshape(lax.axis_size(chip), lax.axis_size("zh"), own_rows, width)
    image_sum = scatter_sum(scatter_sum(image_part, chip), "zh")
    text_part = lax.dot_general(
        weights, img_rows, (((0,), (0,)), ((), ())), preferred_element_type=jnp.float32
    )
    text_part = text_part.reshape(lax.axis_size("y"), lax.axis_size("zl"), own_rows, width)
    text_sum = scatter_sum(scatter_sum(text_part, "y"), "zl")
    grad_image = logit_scale * image_sum - logit_scale * text_emb.astype(jnp.float32)
    grad_text = logit_scale * text_sum - logit_scale * image_emb.astype(jnp.float32)
    own_row = lax.axis_index(chip) * lax.axis_size("zh") + lax.axis_index("zh")
    own_row_lse = lax.dynamic_slice_in_dim(row_lse, own_row * own_rows, own_rows, 0)
    own_col_lse = lax.dynamic_slice_in_dim(col_lse, lax.axis_index(blk) * own_rows, own_rows, 0)
    diag = logit_scale * jnp.sum(
        image_emb.astype(jnp.float32) * text_emb.astype(jnp.float32), axis=1
    )
    row_loss = 0.5 * (own_row_lse + own_col_lse) - diag
    return (grad_image, grad_text, row_loss)


def solution(mesh):
    mesh = Mesh(mesh.devices.reshape(tuple(fine.values())), tuple(fine))
    placed = P(everything, None)
    return jax.shard_map(
        body,
        mesh=mesh,
        in_specs=(placed, placed),
        out_specs=(placed, placed, P(everything)),
        check_vma=False,
    )
```

```python
import functools

import jax
import jax.numpy as jnp
from jax import lax
from jax.sharding import Mesh, PartitionSpec as P

logit_scale = 100.0

fine = {"y": 4, "zl": 8, "zh": 4, "x": 4, "core": 2}
chip = ("x", "core")
dp = ("zh", "x", "core")
blk = ("y", "zl")
everything = ("y", "zl", "zh", "x", "core")


def gather(rows, axis):
    copies = jnp.broadcast_to(rows[None], (lax.axis_size(axis),) + rows.shape)
    return lax.all_to_all(copies, axis, 0, 0)


def swap(value, axis, step):
    return lax.ppermute(value, axis, [(i, i ^ step) for i in range(lax.axis_size(axis))])


def gather_by_swaps(rows, axis):
    me = lax.axis_index(axis)
    came = [rows] + [swap(rows, axis, p) for p in range(1, lax.axis_size(axis))]
    return jnp.stack([lax.select_n(me ^ k, *came) for k in range(len(came))])


def scatter_sum(parts, axis):
    return jnp.sum(
        lax.all_to_all(parts.astype(jnp.bfloat16), axis, 0, 0).astype(jnp.float32), axis=0
    )


def scatter_sum_by_swaps(parts, axis):
    me = lax.axis_index(axis)
    parts = parts.astype(jnp.bfloat16)
    own = [lax.dynamic_index_in_dim(parts, me ^ p, 0, False) for p in range(parts.shape[0])]
    came = own[:1] + [swap(own[p], axis, p) for p in range(1, parts.shape[0])]
    return sum(part.astype(jnp.float32) for part in came)


def lse(values, dim):
    top = jnp.max(values, axis=dim, keepdims=True)
    return jnp.squeeze(top, dim) + jnp.log(jnp.sum(jnp.exp(values - top), axis=dim))


def lse_of(*values):
    top = functools.reduce(jnp.maximum, values)
    return top + jnp.log(sum(jnp.exp(value - top) for value in values))


def lse_rows(scores):
    return lse(gather(lse(scores, 1), dp), 0)


def lse_cols(scores):
    total = lse(scores, 0)
    total = lse_of(total, *(swap(total, "y", step) for step in (1, 2, 3)))
    total = lse_of(total, *(swap(total, "zl", step) for step in (1, 2, 3)))
    return lse_of(total, swap(total, "zl", 4))


def body(image_emb, text_emb):
    own_rows, width = image_emb.shape
    img_rows = gather(gather_by_swaps(image_emb, "zh"), chip)
    txt_cols = gather_by_swaps(gather(text_emb, "zl"), "y")
    row_lanes, col_lanes = img_rows.shape[:-1], txt_cols.shape[:-1]
    img_rows, txt_cols = img_rows.reshape(-1, width), txt_cols.reshape(-1, width)
    scores = logit_scale * jnp.dot(img_rows, txt_cols.T, preferred_element_type=jnp.float32)
    row_lse = lse_rows(scores)
    col_lse = lse_cols(scores)
    weights = (
        0.5 * (jnp.exp(scores - row_lse[:, None]) + jnp.exp(scores - col_lse[None, :]))
    ).astype(jnp.bfloat16)
    image_part = jnp.dot(weights, txt_cols, preferred_element_type=jnp.float32)
    image_part = image_part.reshape(row_lanes + (width,))
    image_sum = scatter_sum_by_swaps(scatter_sum(image_part, chip), "zh")
    text_part = lax.dot_general(
        weights, img_rows, (((0,), (0,)), ((), ())), preferred_element_type=jnp.float32
    )
    text_part = text_part.reshape(col_lanes + (width,))
    text_sum = scatter_sum(scatter_sum_by_swaps(text_part, "y"), "zl")
    grad_image = logit_scale * image_sum - logit_scale * text_emb.astype(jnp.float32)
    grad_text = logit_scale * text_sum - logit_scale * image_emb.astype(jnp.float32)
    own_row = lax.axis_index(chip) * row_lanes[1] + lax.axis_index("zh")
    own_row_lse = lax.dynamic_slice_in_dim(row_lse, own_row * own_rows, own_rows, 0)
    own_col_lse = lax.dynamic_slice_in_dim(col_lse, lax.axis_index(blk) * own_rows, own_rows, 0)
    diag = logit_scale * jnp.sum(
        image_emb.astype(jnp.float32) * text_emb.astype(jnp.float32), axis=1
    )
    row_loss = 0.5 * (own_row_lse + own_col_lse) - diag
    return (grad_image, grad_text, row_loss)


def solution(mesh):
    mesh = Mesh(mesh.devices.reshape(tuple(fine.values())), tuple(fine))
    placed = P(everything, None)
    return jax.shard_map(
        body,
        mesh=mesh,
        in_specs=(placed, placed),
        out_specs=(placed, placed, P(everything)),
        check_vma=False,
    )
```

```python
import jax
import jax.numpy as jnp
from jax import lax
from jax.sharding import Mesh, PartitionSpec as P

logit_scale = 100.0

fine = {"y": 4, "zl": 8, "zh": 4, "x": 4, "core": 2}
chip = ("x", "core")
bits = (4, 2, 1)
everything = ("y", "zl", "zh", "x", "core")


def axes(axis):
    return axis if isinstance(axis, tuple) else (axis,)


def gather(rows, axis):
    copies = jnp.broadcast_to(rows[None], (lax.axis_size(axis),) + rows.shape)
    return lax.all_to_all(copies, axis, 0, 0)


def swap(value, axis, step):
    return lax.ppermute(value, axis, [(i, i ^ step) for i in range(lax.axis_size(axis))])


def gather_by_swaps(rows, axis):
    me = lax.axis_index(axis)
    came = [rows] + [swap(rows, axis, p) for p in range(1, lax.axis_size(axis))]
    return jnp.stack([lax.select_n(me ^ k, *came) for k in range(len(came))])


def scatter_sum(parts, axis):
    return jnp.sum(
        lax.all_to_all(parts.astype(jnp.bfloat16), axis, 0, 0).astype(jnp.float32), axis=0
    )


def scatter_sum_by_swaps(parts, axis):
    me = lax.axis_index(axis)
    parts = parts.astype(jnp.bfloat16)
    own = [lax.dynamic_index_in_dim(parts, me ^ p, 0, False) for p in range(parts.shape[0])]
    came = own[:1] + [swap(own[p], axis, p) for p in range(1, parts.shape[0])]
    return sum(part.astype(jnp.float32) for part in came)


def lse(values, dim):
    top = jnp.max(values, axis=dim, keepdims=True)
    return jnp.squeeze(top, dim) + jnp.log(jnp.sum(jnp.exp(values - top), axis=dim))


def gather_by_doubling(rows, axis, steps):
    for step in steps:
        other = swap(rows, axis, step)
        upper = (lax.axis_index(axis) & step) != 0
        rows = jnp.stack([jnp.where(upper, other, rows), jnp.where(upper, rows, other)])
    return rows


def scatter_sum_by_halving(parts, axis, steps):
    for step in reversed(steps):
        upper = jnp.where((lax.axis_index(axis) & step) != 0, 1, 0)
        given = swap(lax.dynamic_index_in_dim(parts, 1 - upper, 0, False), axis, step)
        parts = lax.dynamic_index_in_dim(parts, upper, 0, False) + given
    return parts


def lse_over(row, col, row_axis, col_axis):
    n_row, n_col = lax.axis_size(row_axis), lax.axis_size(col_axis)
    here, there = lax.axis_index(col_axis), lax.axis_index(row_axis)
    same = (jnp.arange(n_col) == here)[:, None, None]
    sent = jnp.broadcast_to(jnp.where(same, row, col), (n_col, n_row, row.shape[0]))
    came = lax.all_to_all(sent.reshape(-1, row.shape[0]), axes(col_axis) + axes(row_axis), 0, 0)
    came = came.reshape(sent.shape)
    rows = lax.dynamic_index_in_dim(came, here, 0, False)
    cols = lax.dynamic_index_in_dim(came, there, 1, False)
    cols = jnp.where((jnp.arange(n_col) == here)[:, None], col, cols)
    return lse(rows, 0), lse(cols, 0)


def body(image_emb, text_emb):
    own_rows, width = image_emb.shape
    img_rows = gather(gather(image_emb, "zh"), chip)
    txt_cols = gather_by_swaps(gather_by_doubling(text_emb, "zl", bits), "y")
    row_lanes, col_lanes = img_rows.shape[:-1], txt_cols.shape[:-1]
    img_rows, txt_cols = img_rows.reshape(-1, width), txt_cols.reshape(-1, width)
    scores = logit_scale * jnp.dot(img_rows, txt_cols.T, preferred_element_type=jnp.float32)
    row_lse, col_lse = lse_over(lse(scores, 1), lse(scores, 0), chip, "y")
    row_lse, col_lse = lse_over(row_lse, col_lse, "zh", "zl")
    weights = (
        0.5 * (jnp.exp(scores - row_lse[:, None]) + jnp.exp(scores - col_lse[None, :]))
    ).astype(jnp.bfloat16)
    image_part = jnp.dot(weights, txt_cols, preferred_element_type=jnp.float32)
    image_part = image_part.reshape(row_lanes + (width,))
    image_sum = scatter_sum(scatter_sum(image_part, chip), "zh")
    text_part = lax.dot_general(
        weights, img_rows, (((0,), (0,)), ((), ())), preferred_element_type=jnp.float32
    )
    text_part = text_part.reshape(col_lanes + (width,))
    text_sum = scatter_sum_by_halving(scatter_sum_by_swaps(text_part, "y"), "zl", bits)
    grad_image = logit_scale * image_sum - logit_scale * text_emb.astype(jnp.float32)
    grad_text = logit_scale * text_sum - logit_scale * image_emb.astype(jnp.float32)
    own_row = lax.axis_index(chip) * row_lanes[1] + lax.axis_index("zh")
    own_row_lse = lax.dynamic_slice_in_dim(row_lse, own_row * own_rows, own_rows, 0)
    zl = lax.axis_index("zl")
    own_col = lax.axis_index("y") * 8 + (zl & 1) * 4 + (zl & 2) + (zl >> 2)
    own_col_lse = lax.dynamic_slice_in_dim(col_lse, own_col * own_rows, own_rows, 0)
    diag = logit_scale * jnp.sum(
        image_emb.astype(jnp.float32) * text_emb.astype(jnp.float32), axis=1
    )
    row_loss = 0.5 * (own_row_lse + own_col_lse) - diag
    return (grad_image, grad_text, row_loss)


def solution(mesh):
    mesh = Mesh(mesh.devices.reshape(tuple(fine.values())), tuple(fine))
    placed = P(everything, None)
    return jax.shard_map(
        body,
        mesh=mesh,
        in_specs=(placed, placed),
        out_specs=(placed, placed, P(everything)),
        check_vma=False,
    )
```

```python
import functools

import jax
import jax.numpy as jnp
from jax import lax
from jax.sharding import Mesh, PartitionSpec as P

logit_scale = 100.0

fine = {"y": 4, "zl": 8, "zh": 4, "x": 4, "core": 2}
chip = ("x", "core")
blk = ("y", "zl")
bits = (4, 2, 1)
everything = ("y", "zl", "zh", "x", "core")


def gather(rows, axis):
    copies = jnp.broadcast_to(rows[None], (lax.axis_size(axis),) + rows.shape)
    return lax.all_to_all(copies, axis, 0, 0)


def swap(value, axis, step):
    return lax.ppermute(value, axis, [(i, i ^ step) for i in range(lax.axis_size(axis))])


def gather_by_swaps(rows, axis):
    me = lax.axis_index(axis)
    came = [rows] + [swap(rows, axis, p) for p in range(1, lax.axis_size(axis))]
    return jnp.stack([lax.select_n(me ^ k, *came) for k in range(len(came))])


def scatter_sum(parts, axis):
    return jnp.sum(
        lax.all_to_all(parts.astype(jnp.bfloat16), axis, 0, 0).astype(jnp.float32), axis=0
    )


def scatter_sum_by_swaps(parts, axis):
    me = lax.axis_index(axis)
    parts = parts.astype(jnp.bfloat16)
    own = [lax.dynamic_index_in_dim(parts, me ^ p, 0, False) for p in range(parts.shape[0])]
    came = own[:1] + [swap(own[p], axis, p) for p in range(1, parts.shape[0])]
    return sum(part.astype(jnp.float32) for part in came)


def lse(values, dim):
    top = jnp.max(values, axis=dim, keepdims=True)
    return jnp.squeeze(top, dim) + jnp.log(jnp.sum(jnp.exp(values - top), axis=dim))


def gather_by_doubling(rows, axis, steps):
    for step in steps:
        other = swap(rows, axis, step)
        upper = (lax.axis_index(axis) & step) != 0
        rows = jnp.stack([jnp.where(upper, other, rows), jnp.where(upper, rows, other)])
    return rows


def scatter_sum_by_halving(parts, axis, steps):
    for step in reversed(steps):
        upper = jnp.where((lax.axis_index(axis) & step) != 0, 1, 0)
        given = lax.dynamic_index_in_dim(parts, 1 - upper, 0, False)
        if given.ndim > 2:
            given = given.astype(jnp.bfloat16)
        given = swap(given, axis, step).astype(jnp.float32)
        parts = lax.dynamic_index_in_dim(parts, upper, 0, False) + given
    return parts


def lse_of(*values):
    top = functools.reduce(jnp.maximum, values)
    return top + jnp.log(sum(jnp.exp(value - top) for value in values))


def lse_rows_cols(row, col):
    col = lse(gather(col, blk), 0)
    row = lse_of(row, swap(row, "core", 1))
    row = lse_of(row, *(swap(row, "x", step) for step in (1, 2, 3)))
    row, col = lax.optimization_barrier((row, col))
    return lse(gather(row, "zh"), 0), col


def body(image_emb, text_emb):
    own_rows, width = image_emb.shape
    img_rows = gather(gather(image_emb, "zh"), chip)
    txt_cols = gather_by_swaps(gather_by_doubling(text_emb, "zl", bits), "y")
    row_lanes, col_lanes = img_rows.shape[:-1], txt_cols.shape[:-1]
    img_rows, txt_cols = img_rows.reshape(-1, width), txt_cols.reshape(-1, width)
    scores = logit_scale * jnp.dot(img_rows, txt_cols.T, preferred_element_type=jnp.float32)
    row_lse, col_lse = lse_rows_cols(lse(scores, 1), lse(scores, 0))
    weights = (
        0.5 * (jnp.exp(scores - row_lse[:, None]) + jnp.exp(scores - col_lse[None, :]))
    ).astype(jnp.bfloat16)
    image_part = jnp.dot(weights, txt_cols, preferred_element_type=jnp.float32)
    image_part = image_part.reshape(row_lanes + (width,))
    image_sum = scatter_sum(scatter_sum(image_part, chip), "zh")
    text_part = lax.dot_general(
        weights, img_rows, (((0,), (0,)), ((), ())), preferred_element_type=jnp.float32
    )
    text_part = text_part.reshape(col_lanes + (width,))
    text_sum = scatter_sum_by_halving(scatter_sum_by_swaps(text_part, "y"), "zl", bits)
    grad_image = logit_scale * image_sum - logit_scale * text_emb.astype(jnp.float32)
    grad_text = logit_scale * text_sum - logit_scale * image_emb.astype(jnp.float32)
    own_row = lax.axis_index(chip) * row_lanes[1] + lax.axis_index("zh")
    own_row_lse = lax.dynamic_slice_in_dim(row_lse, own_row * own_rows, own_rows, 0)
    zl = lax.axis_index("zl")
    own_col = lax.axis_index("y") * 8 + (zl & 1) * 4 + (zl & 2) + (zl >> 2)
    own_col_lse = lax.dynamic_slice_in_dim(col_lse, own_col * own_rows, own_rows, 0)
    diag = logit_scale * jnp.sum(
        image_emb.astype(jnp.float32) * text_emb.astype(jnp.float32), axis=1
    )
    row_loss = 0.5 * (own_row_lse + own_col_lse) - diag
    return (grad_image, grad_text, row_loss)


def solution(mesh):
    mesh = Mesh(mesh.devices.reshape(tuple(fine.values())), tuple(fine))
    placed = P(everything, None)
    return jax.shard_map(
        body,
        mesh=mesh,
        in_specs=(placed, placed),
        out_specs=(placed, placed, P(everything)),
        check_vma=False,
    )
```

```python
import functools

import jax
import jax.numpy as jnp
from jax import lax
from jax.sharding import Mesh, PartitionSpec as P

logit_scale = 100.0

fine = {"y": 4, "zl": 8, "zh": 4, "x": 4, "core": 2}
chip = ("x", "core")
blk = ("y", "zl")
ring = ((1, 1), (3, 2))
everything = ("y", "zl", "zh", "x", "core")


def gather(rows, axis):
    copies = jnp.broadcast_to(rows[None], (lax.axis_size(axis),) + rows.shape)
    return lax.all_to_all(copies, axis, 0, 0)


def swap(value, axis, step):
    return lax.ppermute(value, axis, [(i, i ^ step) for i in range(lax.axis_size(axis))])


def gather_by_swaps(rows, axis):
    me = lax.axis_index(axis)
    came = [rows] + [swap(rows, axis, p) for p in range(1, lax.axis_size(axis))]
    return jnp.stack([lax.select_n(me ^ k, *came) for k in range(len(came))])


def scatter_sum(parts, axis):
    return jnp.sum(
        lax.all_to_all(parts.astype(jnp.bfloat16), axis, 0, 0).astype(jnp.float32), axis=0
    )


def scatter_sum_by_swaps(parts, axis):
    me = lax.axis_index(axis)
    parts = parts.astype(jnp.bfloat16)
    own = [lax.dynamic_index_in_dim(parts, me ^ p, 0, False) for p in range(parts.shape[0])]
    came = own[:1] + [swap(own[p], axis, p) for p in range(1, parts.shape[0])]
    return sum(part.astype(jnp.float32) for part in came)


def lse(values, dim):
    top = jnp.max(values, axis=dim, keepdims=True)
    return jnp.squeeze(top, dim) + jnp.log(jnp.sum(jnp.exp(values - top), axis=dim))


def gather_by_doubling(rows, axis, steps):
    for step, bit in steps:
        other = swap(rows, axis, step)
        upper = (lax.axis_index(axis) & bit) != 0
        rows = jnp.stack([jnp.where(upper, other, rows), jnp.where(upper, rows, other)])
    return rows


def scatter_sum_by_halving(parts, axis, steps):
    for step, bit in reversed(steps):
        upper = jnp.where((lax.axis_index(axis) & bit) != 0, 1, 0)
        given = lax.dynamic_index_in_dim(parts, 1 - upper, 0, False).astype(jnp.bfloat16)
        given = swap(given, axis, step).astype(jnp.float32)
        parts = lax.dynamic_index_in_dim(parts, upper, 0, False) + given
    return parts


def lse_of(*values):
    top = functools.reduce(jnp.maximum, values)
    return top + jnp.log(sum(jnp.exp(value - top) for value in values))


def lse_rows_cols(row, col):
    row = lse(gather(row, chip), 0)
    col = lse_of(col, *(swap(col, "y", step) for step in (1, 2, 3)))
    row, col = lax.optimization_barrier((row, col))
    for step, _ in ring:
        row = lse_of(row, swap(row, "zh", step))
    for step in (1, 2, 4):
        col = lse_of(col, swap(col, "zl", step))
    return row, col


def body(image_emb, text_emb):
    own_rows, width = image_emb.shape
    img_rows = gather(gather_by_doubling(image_emb, "zh", ring), chip)
    txt_cols = gather_by_swaps(gather(text_emb, "zl"), "y")
    img_rows = img_rows.reshape(img_rows.shape[0], -1, own_rows, width)
    row_lanes, col_lanes = img_rows.shape[:-1], txt_cols.shape[:-1]
    img_rows, txt_cols = img_rows.reshape(-1, width), txt_cols.reshape(-1, width)
    scores = logit_scale * jnp.dot(img_rows, txt_cols.T, preferred_element_type=jnp.float32)
    row_lse, col_lse = lse_rows_cols(lse(scores, 1), lse(scores, 0))
    weights = (
        0.5 * (jnp.exp(scores - row_lse[:, None]) + jnp.exp(scores - col_lse[None, :]))
    ).astype(jnp.bfloat16)
    image_part = jnp.dot(weights, txt_cols, preferred_element_type=jnp.float32)
    image_part = image_part.reshape(row_lanes + (width,))
    image_sum = scatter_sum(image_part, chip).reshape(2, 2, own_rows, width)
    image_sum = scatter_sum_by_halving(image_sum, "zh", ring)
    text_part = lax.dot_general(
        weights, img_rows, (((0,), (0,)), ((), ())), preferred_element_type=jnp.float32
    )
    text_part = text_part.reshape(col_lanes + (width,))
    text_sum = scatter_sum(scatter_sum_by_swaps(text_part, "y"), "zl")
    grad_image = logit_scale * image_sum - logit_scale * text_emb.astype(jnp.float32)
    grad_text = logit_scale * text_sum - logit_scale * image_emb.astype(jnp.float32)
    own_row = lax.axis_index(chip) * row_lanes[1] + lax.axis_index("zh")
    own_row_lse = lax.dynamic_slice_in_dim(row_lse, own_row * own_rows, own_rows, 0)
    own_col_lse = lax.dynamic_slice_in_dim(col_lse, lax.axis_index(blk) * own_rows, own_rows, 0)
    diag = logit_scale * jnp.sum(
        image_emb.astype(jnp.float32) * text_emb.astype(jnp.float32), axis=1
    )
    row_loss = 0.5 * (own_row_lse + own_col_lse) - diag
    return (grad_image, grad_text, row_loss)


def solution(mesh):
    mesh = Mesh(mesh.devices.reshape(tuple(fine.values())), tuple(fine))
    placed = P(everything, None)
    return jax.shard_map(
        body,
        mesh=mesh,
        in_specs=(placed, placed),
        out_specs=(placed, placed, P(everything)),
        check_vma=False,
    )
```

```python
import functools

import jax
import jax.numpy as jnp
from jax import lax
from jax.sharding import Mesh, PartitionSpec as P

logit_scale = 100.0

fine = {"y": 4, "zl": 8, "zh": 4, "x": 4, "core": 2}
chip = ("x", "core")
far = ("zh", "x")
blk = ("y", "zl")
ring = ((1, 1), (3, 2))
everything = ("y", "zl", "zh", "x", "core")


def gather(rows, axis):
    copies = jnp.broadcast_to(rows[None], (lax.axis_size(axis),) + rows.shape)
    return lax.all_to_all(copies, axis, 0, 0)


def swap(value, axis, step):
    return lax.ppermute(value, axis, [(i, i ^ step) for i in range(lax.axis_size(axis))])


def gather_by_swaps(rows, axis):
    me = lax.axis_index(axis)
    came = [rows] + [swap(rows, axis, p) for p in range(1, lax.axis_size(axis))]
    return jnp.stack([lax.select_n(me ^ k, *came) for k in range(len(came))])


def scatter_sum(parts, axis):
    return jnp.sum(
        lax.all_to_all(parts.astype(jnp.bfloat16), axis, 0, 0).astype(jnp.float32), axis=0
    )


def scatter_sum_by_swaps(parts, axis):
    me = lax.axis_index(axis)
    parts = parts.astype(jnp.bfloat16)
    own = [lax.dynamic_index_in_dim(parts, me ^ p, 0, False) for p in range(parts.shape[0])]
    came = own[:1] + [swap(own[p], axis, p) for p in range(1, parts.shape[0])]
    return sum(part.astype(jnp.float32) for part in came)


def lse(values, dim):
    top = jnp.max(values, axis=dim, keepdims=True)
    return jnp.squeeze(top, dim) + jnp.log(jnp.sum(jnp.exp(values - top), axis=dim))


def gather_by_doubling(rows, axis, steps):
    for step, bit in steps:
        other = swap(rows, axis, step)
        upper = (lax.axis_index(axis) & bit) != 0
        rows = jnp.stack([jnp.where(upper, other, rows), jnp.where(upper, rows, other)])
    return rows


def scatter_sum_by_halving(parts, axis, steps):
    for step, bit in reversed(steps):
        upper = jnp.where((lax.axis_index(axis) & bit) != 0, 1, 0)
        given = lax.dynamic_index_in_dim(parts, 1 - upper, 0, False).astype(jnp.bfloat16)
        given = swap(given, axis, step).astype(jnp.float32)
        parts = lax.dynamic_index_in_dim(parts, upper, 0, False) + given
    return parts


def top_total(scores, dim):
    top = jnp.max(scores, axis=dim, keepdims=True)
    return jnp.squeeze(top, dim), jnp.sum(jnp.exp(scores - top), axis=dim)


def combine(tops, totals):
    top = functools.reduce(jnp.maximum, tops)
    return top, sum(total * jnp.exp(each - top) for each, total in zip(tops, totals))


def lse_of(*values):
    top = functools.reduce(jnp.maximum, values)
    return top + jnp.log(sum(jnp.exp(value - top) for value in values))


def lse_rows_cols(scores):
    every = gather(jnp.stack(top_total(scores, 1)), far)
    col = lse(scores, 0)
    col = lse_of(col, *(swap(col, "y", step) for step in (1, 2, 3)))
    col = lse_of(col, *(swap(col, "zl", step) for step in (1, 2, 3)))
    every, col = lax.optimization_barrier((every, col))
    n = every.shape[0]
    own = jnp.stack(combine([every[k, 0] for k in range(n)], [every[k, 1] for k in range(n)]))
    other = swap(own, "core", 1)
    top, total = combine((own[0], other[0]), (own[1], other[1]))
    return top + jnp.log(total), lse_of(col, swap(col, "zl", 4))


def body(image_emb, text_emb):
    own_rows, width = image_emb.shape
    img_rows = gather(gather_by_doubling(image_emb, "zh", ring), chip)
    txt_cols = gather_by_swaps(gather(text_emb, "zl"), "y")
    img_rows = img_rows.reshape(img_rows.shape[0], -1, own_rows, width)
    row_lanes, col_lanes = img_rows.shape[:-1], txt_cols.shape[:-1]
    img_rows, txt_cols = img_rows.reshape(-1, width), txt_cols.reshape(-1, width)
    scores = logit_scale * jnp.dot(img_rows, txt_cols.T, preferred_element_type=jnp.float32)
    row_lse, col_lse = lse_rows_cols(scores)
    weights = (
        0.5 * (jnp.exp(scores - row_lse[:, None]) + jnp.exp(scores - col_lse[None, :]))
    ).astype(jnp.bfloat16)
    image_part = jnp.dot(weights, txt_cols, preferred_element_type=jnp.float32)
    image_part = image_part.reshape(row_lanes + (width,))
    text_part = lax.dot_general(
        weights, img_rows, (((0,), (0,)), ((), ())), preferred_element_type=jnp.float32
    )
    text_part = text_part.reshape(col_lanes + (width,))
    image_sum = scatter_sum(image_part, chip).reshape(2, 2, own_rows, width)
    text_sum = scatter_sum_by_swaps(text_part, "y")
    image_sum = scatter_sum_by_halving(image_sum, "zh", ring[1:])
    image_sum, text_sum = lax.optimization_barrier((image_sum, text_sum))
    image_sum = scatter_sum_by_halving(image_sum, "zh", ring[:1])
    text_sum = scatter_sum(text_sum, "zl")
    grad_image = logit_scale * image_sum - logit_scale * text_emb.astype(jnp.float32)
    grad_text = logit_scale * text_sum - logit_scale * image_emb.astype(jnp.float32)
    own_row = lax.axis_index(chip) * row_lanes[1] + lax.axis_index("zh")
    own_row_lse = lax.dynamic_slice_in_dim(row_lse, own_row * own_rows, own_rows, 0)
    own_col_lse = lax.dynamic_slice_in_dim(col_lse, lax.axis_index(blk) * own_rows, own_rows, 0)
    diag = logit_scale * jnp.sum(
        image_emb.astype(jnp.float32) * text_emb.astype(jnp.float32), axis=1
    )
    row_loss = 0.5 * (own_row_lse + own_col_lse) - diag
    return (grad_image, grad_text, row_loss)


def solution(mesh):
    mesh = Mesh(mesh.devices.reshape(tuple(fine.values())), tuple(fine))
    placed = P(everything, None)
    return jax.shard_map(
        body,
        mesh=mesh,
        in_specs=(placed, placed),
        out_specs=(placed, placed, P(everything)),
        check_vma=False,
    )
```

```python
import functools

import jax
import jax.numpy as jnp
from jax import lax
from jax.sharding import Mesh, PartitionSpec as P

logit_scale = 100.0

fine = {"y": 4, "zl": 8, "zh": 4, "x": 4, "core": 2}
chip = ("x", "core")
blk = ("y", "zl")
ring = ((1, 1), (3, 2))
everything = ("y", "zl", "zh", "x", "core")


def gather(rows, axis):
    copies = jnp.broadcast_to(rows[None], (lax.axis_size(axis),) + rows.shape)
    return lax.all_to_all(copies, axis, 0, 0)


def swap(value, axis, step):
    return lax.ppermute(value, axis, [(i, i ^ step) for i in range(lax.axis_size(axis))])


def gather_by_swaps(rows, axis):
    me = lax.axis_index(axis)
    came = [rows] + [swap(rows, axis, p) for p in range(1, lax.axis_size(axis))]
    return jnp.stack([lax.select_n(me ^ k, *came) for k in range(len(came))])


def scatter_sum(parts, axis):
    return jnp.sum(
        lax.all_to_all(parts.astype(jnp.bfloat16), axis, 0, 0).astype(jnp.float32), axis=0
    )


def scatter_sum_by_swaps(parts, axis):
    me = lax.axis_index(axis)
    parts = parts.astype(jnp.bfloat16)
    own = [lax.dynamic_index_in_dim(parts, me ^ p, 0, False) for p in range(parts.shape[0])]
    came = own[:1] + [swap(own[p], axis, p) for p in range(1, parts.shape[0])]
    return sum(part.astype(jnp.float32) for part in came)


def lse(values, dim):
    top = jnp.max(values, axis=dim, keepdims=True)
    return jnp.squeeze(top, dim) + jnp.log(jnp.sum(jnp.exp(values - top), axis=dim))


def gather_by_doubling(rows, axis, steps):
    for step, bit in steps:
        other = swap(rows, axis, step)
        upper = (lax.axis_index(axis) & bit) != 0
        rows = jnp.stack([jnp.where(upper, other, rows), jnp.where(upper, rows, other)])
    return rows


def scatter_sum_by_halving(parts, axis, steps):
    for step, bit in reversed(steps):
        upper = jnp.where((lax.axis_index(axis) & bit) != 0, 1, 0)
        given = lax.dynamic_index_in_dim(parts, 1 - upper, 0, False).astype(jnp.bfloat16)
        given = swap(given, axis, step).astype(jnp.float32)
        parts = lax.dynamic_index_in_dim(parts, upper, 0, False) + given
    return parts


def lse_of(*values):
    top = functools.reduce(jnp.maximum, values)
    return top + jnp.log(sum(jnp.exp(value - top) for value in values))


def lse_near(row, col):
    n_y, n_chip = lax.axis_size("y"), lax.axis_size(chip)
    y, own = lax.axis_index("y"), lax.axis_index(chip)
    same = (jnp.arange(n_y) == y)[:, None]
    sent = jnp.where(same, row, col)
    sent = jnp.broadcast_to(sent[:, None], (n_y, n_chip, row.shape[0]))
    came = lax.all_to_all(sent.reshape(-1, row.shape[0]), ("y",) + chip, 0, 0).reshape(sent.shape)
    rows = lax.dynamic_index_in_dim(came, y, 0, False)
    cols = jnp.where(same, col, lax.dynamic_index_in_dim(came, own, 1, False))
    return lse(rows, 0), lse(cols, 0)


def lse_rows_cols(scores):
    row, col = lse_near(lse(scores, 1), lse(scores, 0))
    cols = gather(col, "zl")
    row = lse_of(row, swap(row, "zh", ring[0][0]))
    row, cols = lax.optimization_barrier((row, cols))
    return lse_of(row, swap(row, "zh", ring[1][0])), lse(cols, 0)


def body(image_emb, text_emb):
    own_rows, width = image_emb.shape
    img_rows = gather(gather_by_doubling(image_emb, "zh", ring), chip)
    txt_cols = gather_by_swaps(gather(text_emb, "zl"), "y")
    img_rows = img_rows.reshape(img_rows.shape[0], -1, own_rows, width)
    row_lanes, col_lanes = img_rows.shape[:-1], txt_cols.shape[:-1]
    img_rows, txt_cols = img_rows.reshape(-1, width), txt_cols.reshape(-1, width)
    scores = logit_scale * jnp.dot(img_rows, txt_cols.T, preferred_element_type=jnp.float32)
    row_lse, col_lse = lse_rows_cols(scores)
    weights = (
        0.5 * (jnp.exp(scores - row_lse[:, None]) + jnp.exp(scores - col_lse[None, :]))
    ).astype(jnp.bfloat16)
    image_part = jnp.dot(weights, txt_cols, preferred_element_type=jnp.float32)
    image_part = image_part.reshape(row_lanes + (width,))
    text_part = lax.dot_general(
        weights, img_rows, (((0,), (0,)), ((), ())), preferred_element_type=jnp.float32
    )
    text_part = text_part.reshape(col_lanes + (width,))
    image_sum = scatter_sum(image_part, chip).reshape(2, 2, own_rows, width)
    image_sum = scatter_sum_by_halving(image_sum, "zh", ring)
    text_sum = scatter_sum(scatter_sum_by_swaps(text_part, "y"), "zl")
    grad_image = logit_scale * image_sum - logit_scale * text_emb.astype(jnp.float32)
    grad_text = logit_scale * text_sum - logit_scale * image_emb.astype(jnp.float32)
    own_row = lax.axis_index(chip) * row_lanes[1] + lax.axis_index("zh")
    own_row_lse = lax.dynamic_slice_in_dim(row_lse, own_row * own_rows, own_rows, 0)
    own_col_lse = lax.dynamic_slice_in_dim(col_lse, lax.axis_index(blk) * own_rows, own_rows, 0)
    diag = logit_scale * jnp.sum(
        image_emb.astype(jnp.float32) * text_emb.astype(jnp.float32), axis=1
    )
    row_loss = 0.5 * (own_row_lse + own_col_lse) - diag
    return (grad_image, grad_text, row_loss)


def solution(mesh):
    mesh = Mesh(mesh.devices.reshape(tuple(fine.values())), tuple(fine))
    placed = P(everything, None)
    return jax.shard_map(
        body,
        mesh=mesh,
        in_specs=(placed, placed),
        out_specs=(placed, placed, P(everything)),
        check_vma=False,
    )
```

```python
import functools

import jax
import jax.numpy as jnp
from jax import lax
from jax.sharding import Mesh, PartitionSpec as P

logit_scale = 100.0

fine = {"y": 4, "zl": 8, "zh": 4, "x": 4, "core": 2}
chip = ("x", "core")
dp = ("zh", "x", "core")
blk = ("y", "zl")
ring = ((1, 1), (3, 2))
everything = ("y", "zl", "zh", "x", "core")


def gather(rows, axis):
    copies = jnp.broadcast_to(rows[None], (lax.axis_size(axis),) + rows.shape)
    return lax.all_to_all(copies, axis, 0, 0)


def swap(value, axis, step):
    return lax.ppermute(value, axis, [(i, i ^ step) for i in range(lax.axis_size(axis))])


def gather_by_swaps(rows, axis):
    me = lax.axis_index(axis)
    came = [rows] + [swap(rows, axis, p) for p in range(1, lax.axis_size(axis))]
    return jnp.stack([lax.select_n(me ^ k, *came) for k in range(len(came))])


def scatter_sum(parts, axis):
    return jnp.sum(
        lax.all_to_all(parts.astype(jnp.bfloat16), axis, 0, 0).astype(jnp.float32), axis=0
    )


def scatter_sum_by_swaps(parts, axis):
    me = lax.axis_index(axis)
    parts = parts.astype(jnp.bfloat16)
    own = [lax.dynamic_index_in_dim(parts, me ^ p, 0, False) for p in range(parts.shape[0])]
    came = own[:1] + [swap(own[p], axis, p) for p in range(1, parts.shape[0])]
    return sum(part.astype(jnp.float32) for part in came)


def lse(values, dim):
    top = jnp.max(values, axis=dim, keepdims=True)
    return jnp.squeeze(top, dim) + jnp.log(jnp.sum(jnp.exp(values - top), axis=dim))


def gather_by_doubling(rows, axis, steps):
    for step, bit in steps:
        other = swap(rows, axis, step)
        upper = (lax.axis_index(axis) & bit) != 0
        rows = jnp.stack([jnp.where(upper, other, rows), jnp.where(upper, rows, other)])
    return rows


def scatter_sum_by_halving(parts, axis, steps):
    for step, bit in reversed(steps):
        upper = jnp.where((lax.axis_index(axis) & bit) != 0, 1, 0)
        given = lax.dynamic_index_in_dim(parts, 1 - upper, 0, False).astype(jnp.bfloat16)
        given = swap(given, axis, step).astype(jnp.float32)
        parts = lax.dynamic_index_in_dim(parts, upper, 0, False) + given
    return parts


def lse_of(*values):
    top = functools.reduce(jnp.maximum, values)
    return top + jnp.log(sum(jnp.exp(value - top) for value in values))


def lse_rows_cols(scores):
    cols, row = lax.optimization_barrier((gather(lse(scores, 0), blk), lse(scores, 1)))
    return lse(gather(row, dp), 0), lse(cols, 0)


def weighted(scores, row_lse, col_lse):
    return (
        0.5 * (jnp.exp(scores - row_lse[:, None]) + jnp.exp(scores - col_lse[None, :]))
    ).astype(jnp.bfloat16)


def body(image_emb, text_emb):
    own_rows, width = image_emb.shape
    img_rows = gather(gather_by_doubling(image_emb, "zh", ring), chip)
    txt_cols = gather_by_swaps(gather(text_emb, "zl"), "y")
    img_rows = img_rows.reshape(img_rows.shape[0], -1, own_rows, width)
    row_lanes, col_lanes = img_rows.shape[:-1], txt_cols.shape[:-1]
    img_rows, txt_cols = img_rows.reshape(-1, width), txt_cols.reshape(-1, width)
    scores = logit_scale * jnp.dot(img_rows, txt_cols.T, preferred_element_type=jnp.float32)
    row_lse, col_lse = lse_rows_cols(scores)
    weights = weighted(scores, row_lse, col_lse)
    image_part = jnp.dot(weights, txt_cols, preferred_element_type=jnp.float32)
    image_part = image_part.astype(jnp.bfloat16).reshape(row_lanes + (width,))
    image_part, scores = lax.optimization_barrier((image_part, scores))
    weights = weighted(scores, row_lse, col_lse)
    text_part = lax.dot_general(
        weights, img_rows, (((0,), (0,)), ((), ())), preferred_element_type=jnp.float32
    )
    text_part = text_part.reshape(col_lanes + (width,))
    image_sum = scatter_sum(image_part, chip).reshape(2, 2, own_rows, width)
    image_sum = scatter_sum_by_halving(image_sum, "zh", ring)
    text_sum = scatter_sum(scatter_sum_by_swaps(text_part, "y"), "zl")
    grad_image = logit_scale * image_sum - logit_scale * text_emb.astype(jnp.float32)
    grad_text = logit_scale * text_sum - logit_scale * image_emb.astype(jnp.float32)
    own_row = lax.axis_index(chip) * row_lanes[1] + lax.axis_index("zh")
    own_row_lse = lax.dynamic_slice_in_dim(row_lse, own_row * own_rows, own_rows, 0)
    own_col_lse = lax.dynamic_slice_in_dim(col_lse, lax.axis_index(blk) * own_rows, own_rows, 0)
    image_own, text_own = lax.optimization_barrier((image_emb, text_emb))
    diag = logit_scale * jnp.sum(
        image_own.astype(jnp.float32) * text_own.astype(jnp.float32), axis=1
    )
    row_loss = 0.5 * (own_row_lse + own_col_lse) - diag
    return (grad_image, grad_text, row_loss)


def solution(mesh):
    mesh = Mesh(mesh.devices.reshape(tuple(fine.values())), tuple(fine))
    placed = P(everything, None)
    return jax.shard_map(
        body,
        mesh=mesh,
        in_specs=(placed, placed),
        out_specs=(placed, placed, P(everything)),
        check_vma=False,
    )
```

```python
import functools

import jax
import jax.numpy as jnp
from jax import lax
from jax.sharding import Mesh, PartitionSpec as P

logit_scale = 100.0

fine = {"y": 4, "zl": 8, "zh": 4, "x": 4, "core": 2}
chip = ("x", "core")
blk = ("y", "zl")
ring = ((1, 1), (3, 2))
everything = ("y", "zl", "zh", "x", "core")


def gather(rows, axis):
    copies = jnp.broadcast_to(rows[None], (lax.axis_size(axis),) + rows.shape)
    return lax.all_to_all(copies, axis, 0, 0)


def swap(value, axis, step):
    return lax.ppermute(value, axis, [(i, i ^ step) for i in range(lax.axis_size(axis))])


def gather_by_swaps(rows, axis):
    me = lax.axis_index(axis)
    came = [rows] + [swap(rows, axis, p) for p in range(1, lax.axis_size(axis))]
    return jnp.stack([lax.select_n(me ^ k, *came) for k in range(len(came))])


def scatter_sum(parts, axis):
    return jnp.sum(
        lax.all_to_all(parts.astype(jnp.bfloat16), axis, 0, 0).astype(jnp.float32), axis=0
    )


def scatter_sum_by_swaps(parts, axis):
    me = lax.axis_index(axis)
    parts = parts.astype(jnp.bfloat16)
    own = [lax.dynamic_index_in_dim(parts, me ^ p, 0, False) for p in range(parts.shape[0])]
    came = own[:1] + [swap(own[p], axis, p) for p in range(1, parts.shape[0])]
    return sum(part.astype(jnp.float32) for part in came)


def lse(values, dim):
    top = jnp.max(values, axis=dim, keepdims=True)
    return jnp.squeeze(top, dim) + jnp.log(jnp.sum(jnp.exp(values - top), axis=dim))


def gather_by_doubling(rows, axis, steps):
    for step, bit in steps:
        other = swap(rows, axis, step)
        upper = (lax.axis_index(axis) & bit) != 0
        rows = jnp.stack([jnp.where(upper, other, rows), jnp.where(upper, rows, other)])
    return rows


def scatter_sum_by_halving(parts, axis, steps):
    for step, bit in reversed(steps):
        upper = jnp.where((lax.axis_index(axis) & bit) != 0, 1, 0)
        given = lax.dynamic_index_in_dim(parts, 1 - upper, 0, False).astype(jnp.bfloat16)
        given = swap(given, axis, step).astype(jnp.float32)
        parts = lax.dynamic_index_in_dim(parts, upper, 0, False) + given
    return parts


def lse_of(*values):
    top = functools.reduce(jnp.maximum, values)
    return top + jnp.log(sum(jnp.exp(value - top) for value in values))


def lse_near(row, col):
    n_zl, n_chip = lax.axis_size("zl"), lax.axis_size(chip)
    zl, own = lax.axis_index("zl"), lax.axis_index(chip)
    same = (jnp.arange(n_zl) == zl)[:, None]
    sent = jnp.where(same, row, col)
    sent = jnp.broadcast_to(sent[:, None], (n_zl, n_chip, row.shape[0]))
    came = lax.all_to_all(sent.reshape(-1, row.shape[0]), ("zl",) + chip, 0, 0).reshape(sent.shape)
    rows = lax.dynamic_index_in_dim(came, zl, 0, False)
    cols = jnp.where(same, col, lax.dynamic_index_in_dim(came, own, 1, False))
    return lse(rows, 0), lse(cols, 0)


def lse_rows_cols(scores):
    row, col = lse_near(lse(scores, 1), lse(scores, 0))
    for step, _ in ring:
        row = lse_of(row, swap(row, "zh", step))
    return row, lse_of(col, *(swap(col, "y", step) for step in (1, 2, 3)))


def body(image_emb, text_emb):
    own_rows, width = image_emb.shape
    img_rows = gather(gather_by_doubling(image_emb, "zh", ring), chip)
    txt_cols = gather_by_swaps(gather(text_emb, "zl"), "y")
    img_rows = img_rows.reshape(img_rows.shape[0], -1, own_rows, width)
    row_lanes, col_lanes = img_rows.shape[:-1], txt_cols.shape[:-1]
    img_rows, txt_cols = img_rows.reshape(-1, width), txt_cols.reshape(-1, width)
    scores = logit_scale * jnp.dot(img_rows, txt_cols.T, preferred_element_type=jnp.float32)
    row_lse, col_lse = lse_rows_cols(scores)
    weights = (
        0.5 * (jnp.exp(scores - row_lse[:, None]) + jnp.exp(scores - col_lse[None, :]))
    ).astype(jnp.bfloat16)
    image_part = jnp.dot(weights, txt_cols, preferred_element_type=jnp.float32)
    image_part = image_part.reshape(row_lanes + (width,))
    text_part = lax.dot_general(
        weights, img_rows, (((0,), (0,)), ((), ())), preferred_element_type=jnp.float32
    )
    text_part = text_part.reshape(col_lanes + (width,))
    image_sum = scatter_sum(image_part, chip).reshape(2, 2, own_rows, width)
    image_sum = scatter_sum_by_halving(image_sum, "zh", ring)
    text_sum = scatter_sum(scatter_sum_by_swaps(text_part, "y"), "zl")
    grad_image = logit_scale * image_sum - logit_scale * text_emb.astype(jnp.float32)
    grad_text = logit_scale * text_sum - logit_scale * image_emb.astype(jnp.float32)
    own_row = lax.axis_index(chip) * row_lanes[1] + lax.axis_index("zh")
    own_row_lse = lax.dynamic_slice_in_dim(row_lse, own_row * own_rows, own_rows, 0)
    own_col_lse = lax.dynamic_slice_in_dim(col_lse, lax.axis_index(blk) * own_rows, own_rows, 0)
    image_own, text_own = lax.optimization_barrier((image_emb, text_emb))
    diag = logit_scale * jnp.sum(
        image_own.astype(jnp.float32) * text_own.astype(jnp.float32), axis=1
    )
    row_loss = 0.5 * (own_row_lse + own_col_lse) - diag
    return (grad_image, grad_text, row_loss)


def solution(mesh):
    mesh = Mesh(mesh.devices.reshape(tuple(fine.values())), tuple(fine))
    placed = P(everything, None)
    return jax.shard_map(
        body,
        mesh=mesh,
        in_specs=(placed, placed),
        out_specs=(placed, placed, P(everything)),
        check_vma=False,
    )
```

```python
import functools

import jax
import jax.numpy as jnp
from jax import lax
from jax.sharding import Mesh, PartitionSpec as P

logit_scale = 100.0

fine = {"y": 4, "zl": 8, "zh": 4, "x": 4, "core": 2}
chip = ("x", "core")
blk = ("y", "zl")
ring = ((1, 1), (3, 2))
everything = ("y", "zl", "zh", "x", "core")


def gather(rows, axis):
    copies = jnp.broadcast_to(rows[None], (lax.axis_size(axis),) + rows.shape)
    return lax.all_to_all(copies, axis, 0, 0)


def swap(value, axis, step):
    return lax.ppermute(value, axis, [(i, i ^ step) for i in range(lax.axis_size(axis))])


def gather_by_swaps(rows, axis):
    me = lax.axis_index(axis)
    came = [rows] + [swap(rows, axis, p) for p in range(1, lax.axis_size(axis))]
    return jnp.stack([lax.select_n(me ^ k, *came) for k in range(len(came))])


def scatter_sum(parts, axis):
    return jnp.sum(
        lax.all_to_all(parts.astype(jnp.bfloat16), axis, 0, 0).astype(jnp.float32), axis=0
    )


def scatter_sum_by_swaps(parts, axis):
    me = lax.axis_index(axis)
    parts = parts.astype(jnp.bfloat16)
    own = [lax.dynamic_index_in_dim(parts, me ^ p, 0, False) for p in range(parts.shape[0])]
    came = own[:1] + [swap(own[p], axis, p) for p in range(1, parts.shape[0])]
    return sum(part.astype(jnp.float32) for part in came)


def gather_ring(rows):
    me, half = lax.axis_index("zh"), rows.shape[-1] // 2
    first = gather_by_doubling(rows[:, :half], "zh", me, ring)
    second = gather_by_doubling(rows[:, half:], "zh", me ^ (me >> 1), ring[::-1])
    first = first.reshape((-1,) + first.shape[2:])
    second = jnp.stack([second[0, 0], second[1, 0], second[1, 1], second[0, 1]])
    return jnp.concatenate([first, second], axis=-1)


def scatter_sum_ring(parts):
    me, half = lax.axis_index("zh"), parts.shape[-1] // 2
    first, second = parts[:, :, :half], parts[:, :, half:]
    first = jnp.stack([jnp.stack([first[0], first[1]]), jnp.stack([first[2], first[3]])])
    second = jnp.stack([jnp.stack([second[0], second[3]]), jnp.stack([second[1], second[2]])])
    first = scatter_sum_by_halving(first, "zh", me, ring)
    second = scatter_sum_by_halving(second, "zh", me ^ (me >> 1), ring[::-1])
    return jnp.concatenate([first, second], axis=-1)


def lse(values, dim):
    top = jnp.max(values, axis=dim, keepdims=True)
    return jnp.squeeze(top, dim) + jnp.log(jnp.sum(jnp.exp(values - top), axis=dim))


def gather_by_doubling(rows, axis, code, steps):
    for step, bit in steps:
        other = swap(rows, axis, step)
        upper = (code & bit) != 0
        rows = jnp.stack([jnp.where(upper, other, rows), jnp.where(upper, rows, other)])
    return rows


def scatter_sum_by_halving(parts, axis, code, steps):
    for step, bit in reversed(steps):
        upper = jnp.where((code & bit) != 0, 1, 0)
        given = lax.dynamic_index_in_dim(parts, 1 - upper, 0, False).astype(jnp.bfloat16)
        given = swap(given, axis, step).astype(jnp.float32)
        parts = lax.dynamic_index_in_dim(parts, upper, 0, False) + given
    return parts


def lse_of(*values):
    top = functools.reduce(jnp.maximum, values)
    return top + jnp.log(sum(jnp.exp(value - top) for value in values))


def lse_near(row, col):
    n_y, n_chip = lax.axis_size("y"), lax.axis_size(chip)
    y, own = lax.axis_index("y"), lax.axis_index(chip)
    same = (jnp.arange(n_y) == y)[:, None]
    sent = jnp.where(same, row, col)
    sent = jnp.broadcast_to(sent[:, None], (n_y, n_chip, row.shape[0]))
    came = lax.all_to_all(sent.reshape(-1, row.shape[0]), ("y",) + chip, 0, 0).reshape(sent.shape)
    rows = lax.dynamic_index_in_dim(came, y, 0, False)
    cols = jnp.where(same, col, lax.dynamic_index_in_dim(came, own, 1, False))
    return lse(rows, 0), lse(cols, 0)


def lse_rows_cols(scores):
    row, col = lse_near(lse(scores, 1), lse(scores, 0))
    cols = gather(col, "zl")
    row = lse_of(row, swap(row, "zh", ring[0][0]))
    row, cols = lax.optimization_barrier((row, cols))
    return lse_of(row, swap(row, "zh", ring[1][0])), lse(cols, 0)


def body(image_emb, text_emb):
    own_rows, width = image_emb.shape
    img_rows = gather(gather_ring(image_emb), chip)
    txt_cols = gather_by_swaps(gather(text_emb, "zl"), "y")
    img_rows = img_rows.reshape(img_rows.shape[0], -1, own_rows, width)
    row_lanes, col_lanes = img_rows.shape[:-1], txt_cols.shape[:-1]
    img_rows, txt_cols = img_rows.reshape(-1, width), txt_cols.reshape(-1, width)
    scores = logit_scale * jnp.dot(img_rows, txt_cols.T, preferred_element_type=jnp.float32)
    row_lse, col_lse = lse_rows_cols(scores)
    weights = (
        0.5 * (jnp.exp(scores - row_lse[:, None]) + jnp.exp(scores - col_lse[None, :]))
    ).astype(jnp.bfloat16)
    image_part = jnp.dot(weights, txt_cols, preferred_element_type=jnp.float32)
    image_part = image_part.reshape(row_lanes + (width,))
    text_part = lax.dot_general(
        weights, img_rows, (((0,), (0,)), ((), ())), preferred_element_type=jnp.float32
    )
    text_part = text_part.reshape(col_lanes + (width,))
    image_sum = scatter_sum_ring(scatter_sum(image_part, chip))
    text_sum = scatter_sum(scatter_sum_by_swaps(text_part, "y"), "zl")
    grad_image = logit_scale * image_sum - logit_scale * text_emb.astype(jnp.float32)
    grad_text = logit_scale * text_sum - logit_scale * image_emb.astype(jnp.float32)
    own_row = lax.axis_index(chip) * row_lanes[1] + lax.axis_index("zh")
    own_row_lse = lax.dynamic_slice_in_dim(row_lse, own_row * own_rows, own_rows, 0)
    own_col_lse = lax.dynamic_slice_in_dim(col_lse, lax.axis_index(blk) * own_rows, own_rows, 0)
    image_own, text_own = lax.optimization_barrier((image_emb, text_emb))
    diag = logit_scale * jnp.sum(
        image_own.astype(jnp.float32) * text_own.astype(jnp.float32), axis=1
    )
    row_loss = 0.5 * (own_row_lse + own_col_lse) - diag
    return (grad_image, grad_text, row_loss)


def solution(mesh):
    mesh = Mesh(mesh.devices.reshape(tuple(fine.values())), tuple(fine))
    placed = P(everything, None)
    return jax.shard_map(
        body,
        mesh=mesh,
        in_specs=(placed, placed),
        out_specs=(placed, placed, P(everything)),
        check_vma=False,
    )
```

```python
import functools

import jax
import jax.numpy as jnp
from jax import lax
from jax.sharding import Mesh, PartitionSpec as P

logit_scale = 100.0

fine = {"y": 4, "zl": 8, "zh": 4, "x": 4, "core": 2}
chip = ("x", "core")
dp = ("zh", "x", "core")
blk = ("y", "zl")
ring = ((1, 1), (3, 2))
everything = ("y", "zl", "zh", "x", "core")


def gather(rows, axis):
    copies = jnp.broadcast_to(rows[None], (lax.axis_size(axis),) + rows.shape)
    return lax.all_to_all(copies, axis, 0, 0)


def swap(value, axis, step):
    return lax.ppermute(value, axis, [(i, i ^ step) for i in range(lax.axis_size(axis))])


def gather_by_swaps(rows, axis):
    me = lax.axis_index(axis)
    came = [rows] + [swap(rows, axis, p) for p in range(1, lax.axis_size(axis))]
    return jnp.stack([lax.select_n(me ^ k, *came) for k in range(len(came))])


def scatter_sum(parts, axis):
    return jnp.sum(
        lax.all_to_all(parts.astype(jnp.bfloat16), axis, 0, 0).astype(jnp.float32), axis=0
    )


def scatter_sum_by_swaps(parts, axis):
    me = lax.axis_index(axis)
    parts = parts.astype(jnp.bfloat16)
    own = [lax.dynamic_index_in_dim(parts, me ^ p, 0, False) for p in range(parts.shape[0])]
    came = own[:1] + [swap(own[p], axis, p) for p in range(1, parts.shape[0])]
    return sum(part.astype(jnp.float32) for part in came)


def lse(values, dim):
    top = jnp.max(values, axis=dim, keepdims=True)
    return jnp.squeeze(top, dim) + jnp.log(jnp.sum(jnp.exp(values - top), axis=dim))


def gather_by_doubling(rows, axis, steps):
    for step, bit in steps:
        other = swap(rows, axis, step)
        upper = (lax.axis_index(axis) & bit) != 0
        rows = jnp.stack([jnp.where(upper, other, rows), jnp.where(upper, rows, other)])
    return rows


def scatter_sum_by_halving(parts, axis, steps):
    for step, bit in reversed(steps):
        upper = jnp.where((lax.axis_index(axis) & bit) != 0, 1, 0)
        given = lax.dynamic_index_in_dim(parts, 1 - upper, 0, False).astype(jnp.bfloat16)
        given = swap(given, axis, step).astype(jnp.float32)
        parts = lax.dynamic_index_in_dim(parts, upper, 0, False) + given
    return parts


def lse_of(*values):
    top = functools.reduce(jnp.maximum, values)
    return top + jnp.log(sum(jnp.exp(value - top) for value in values))


def lse_rows(scores):
    return lse(gather(lse(scores, 1), dp), 0)


def lse_cols(scores):
    col = lse(scores, 0)
    col = lse_of(col, *(swap(col, "y", step) for step in (1, 2, 3)))
    col = lse_of(col, *(swap(col, "zl", step) for step in (1, 2, 3)))
    return lse_of(col, swap(col, "zl", 4))


def body(image_emb, text_emb):
    own_rows, width = image_emb.shape
    img_rows = gather_by_doubling(image_emb, "zh", ring[:1])
    img_rows, txt_cols = lax.optimization_barrier((img_rows, text_emb))
    img_rows = gather(gather_by_doubling(img_rows, "zh", ring[1:]), chip)
    txt_cols = gather_by_swaps(gather(txt_cols, "zl"), "y")
    img_rows = img_rows.reshape(img_rows.shape[0], -1, own_rows, width)
    row_lanes, col_lanes = img_rows.shape[:-1], txt_cols.shape[:-1]
    img_rows, txt_cols = img_rows.reshape(-1, width), txt_cols.reshape(-1, width)
    scores = logit_scale * jnp.dot(img_rows, txt_cols.T, preferred_element_type=jnp.float32)
    row_lse, col_lse = lse_rows(scores), lse_cols(scores)
    weights = (
        0.5 * (jnp.exp(scores - row_lse[:, None]) + jnp.exp(scores - col_lse[None, :]))
    ).astype(jnp.bfloat16)
    image_part = jnp.dot(weights, txt_cols, preferred_element_type=jnp.float32)
    image_part = image_part.reshape(row_lanes + (width,))
    text_part = lax.dot_general(
        weights, img_rows, (((0,), (0,)), ((), ())), preferred_element_type=jnp.float32
    )
    text_part = text_part.reshape(col_lanes + (width,))
    image_sum = scatter_sum(image_part, chip).reshape(2, 2, own_rows, width)
    image_sum = scatter_sum_by_halving(image_sum, "zh", ring)
    text_sum = scatter_sum(scatter_sum_by_swaps(text_part, "y"), "zl")
    grad_image = logit_scale * image_sum - logit_scale * text_emb.astype(jnp.float32)
    grad_text = logit_scale * text_sum - logit_scale * image_emb.astype(jnp.float32)
    own_row = lax.axis_index(chip) * row_lanes[1] + lax.axis_index("zh")
    own_row_lse = lax.dynamic_slice_in_dim(row_lse, own_row * own_rows, own_rows, 0)
    own_col_lse = lax.dynamic_slice_in_dim(col_lse, lax.axis_index(blk) * own_rows, own_rows, 0)
    image_own, text_own = lax.optimization_barrier((image_emb, text_emb))
    diag = logit_scale * jnp.sum(
        image_own.astype(jnp.float32) * text_own.astype(jnp.float32), axis=1
    )
    row_loss = 0.5 * (own_row_lse + own_col_lse) - diag
    return (grad_image, grad_text, row_loss)


def solution(mesh):
    mesh = Mesh(mesh.devices.reshape(tuple(fine.values())), tuple(fine))
    placed = P(everything, None)
    return jax.shard_map(
        body,
        mesh=mesh,
        in_specs=(placed, placed),
        out_specs=(placed, placed, P(everything)),
        check_vma=False,
    )
```

```python
import jax
import jax.numpy as jnp
from jax import lax
from jax.sharding import Mesh, PartitionSpec as P

logit_scale = 100.0

fine = {"y": 4, "zl": 8, "zh": 4, "x": 4, "core": 2}
chip = ("x", "core")
blk = ("y", "zl")
ring = ((1, 1), (3, 2))
everything = ("y", "zl", "zh", "x", "core")


def axes(axis):
    return axis if isinstance(axis, tuple) else (axis,)


def gather(rows, axis):
    copies = jnp.broadcast_to(rows[None], (lax.axis_size(axis),) + rows.shape)
    return lax.all_to_all(copies, axis, 0, 0)


def swap(value, axis, step):
    return lax.ppermute(value, axis, [(i, i ^ step) for i in range(lax.axis_size(axis))])


def gather_by_swaps(rows, axis):
    me = lax.axis_index(axis)
    came = [rows] + [swap(rows, axis, p) for p in range(1, lax.axis_size(axis))]
    return jnp.stack([lax.select_n(me ^ k, *came) for k in range(len(came))])


def scatter_sum(parts, axis):
    return jnp.sum(
        lax.all_to_all(parts.astype(jnp.bfloat16), axis, 0, 0).astype(jnp.float32), axis=0
    )


def scatter_sum_by_swaps(parts, axis):
    me = lax.axis_index(axis)
    parts = parts.astype(jnp.bfloat16)
    own = [lax.dynamic_index_in_dim(parts, me ^ p, 0, False) for p in range(parts.shape[0])]
    came = own[:1] + [swap(own[p], axis, p) for p in range(1, parts.shape[0])]
    return sum(part.astype(jnp.float32) for part in came)


def lse(values, dim):
    top = jnp.max(values, axis=dim, keepdims=True)
    return jnp.squeeze(top, dim) + jnp.log(jnp.sum(jnp.exp(values - top), axis=dim))


def gather_by_doubling(rows, axis, steps):
    for step, bit in steps:
        other = swap(rows, axis, step)
        upper = (lax.axis_index(axis) & bit) != 0
        rows = jnp.stack([jnp.where(upper, other, rows), jnp.where(upper, rows, other)])
    return rows


def scatter_sum_by_halving(parts, axis, steps):
    for step, bit in reversed(steps):
        upper = jnp.where((lax.axis_index(axis) & bit) != 0, 1, 0)
        given = lax.dynamic_index_in_dim(parts, 1 - upper, 0, False).astype(jnp.bfloat16)
        given = swap(given, axis, step).astype(jnp.float32)
        parts = lax.dynamic_index_in_dim(parts, upper, 0, False) + given
    return parts


def lse_over(row, col, row_axis, col_axis):
    n_row, n_col = lax.axis_size(row_axis), lax.axis_size(col_axis)
    here, there = lax.axis_index(col_axis), lax.axis_index(row_axis)
    same = (jnp.arange(n_col) == here)[:, None, None]
    sent = jnp.broadcast_to(jnp.where(same, row, col), (n_col, n_row, row.shape[0]))
    came = lax.all_to_all(sent.reshape(-1, row.shape[0]), axes(col_axis) + axes(row_axis), 0, 0)
    came = came.reshape(sent.shape)
    rows = lax.dynamic_index_in_dim(came, here, 0, False)
    cols = lax.dynamic_index_in_dim(came, there, 1, False)
    cols = jnp.where((jnp.arange(n_col) == here)[:, None], col, cols)
    return lse(rows, 0), lse(cols, 0)


def body(image_emb, text_emb):
    own_rows, width = image_emb.shape
    img_rows = gather(gather_by_doubling(image_emb, "zh", ring), chip)
    txt_cols = gather_by_swaps(gather(text_emb, "zl"), "y")
    img_rows = img_rows.reshape(img_rows.shape[0], -1, own_rows, width)
    row_lanes, col_lanes = img_rows.shape[:-1], txt_cols.shape[:-1]
    img_rows, txt_cols = img_rows.reshape(-1, width), txt_cols.reshape(-1, width)
    scores = logit_scale * jnp.dot(img_rows, txt_cols.T, preferred_element_type=jnp.float32)
    row_lse, col_lse = lse_over(lse(scores, 1), lse(scores, 0), chip, "y")
    row_lse, col_lse = lse_over(row_lse, col_lse, "zh", "zl")
    weights = (
        0.5 * (jnp.exp(scores - row_lse[:, None]) + jnp.exp(scores - col_lse[None, :]))
    ).astype(jnp.bfloat16)
    image_part = jnp.dot(weights, txt_cols, preferred_element_type=jnp.float32)
    image_part = image_part.reshape(row_lanes + (width,))
    text_part = lax.dot_general(
        weights, img_rows, (((0,), (0,)), ((), ())), preferred_element_type=jnp.float32
    )
    text_part = text_part.reshape(col_lanes + (width,))
    image_sum = scatter_sum(image_part, chip).reshape(2, 2, own_rows, width)
    image_sum = scatter_sum_by_halving(image_sum, "zh", ring)
    text_sum = scatter_sum(scatter_sum_by_swaps(text_part, "y"), "zl")
    grad_image = logit_scale * image_sum - logit_scale * text_emb.astype(jnp.float32)
    grad_text = logit_scale * text_sum - logit_scale * image_emb.astype(jnp.float32)
    own_row = lax.axis_index(chip) * row_lanes[1] + lax.axis_index("zh")
    own_row_lse = lax.dynamic_slice_in_dim(row_lse, own_row * own_rows, own_rows, 0)
    own_col_lse = lax.dynamic_slice_in_dim(col_lse, lax.axis_index(blk) * own_rows, own_rows, 0)
    image_own, text_own = lax.optimization_barrier((image_emb, text_emb))
    diag = logit_scale * jnp.sum(
        image_own.astype(jnp.float32) * text_own.astype(jnp.float32), axis=1
    )
    row_loss = 0.5 * (own_row_lse + own_col_lse) - diag
    return (grad_image, grad_text, row_loss)


def solution(mesh):
    mesh = Mesh(mesh.devices.reshape(tuple(fine.values())), tuple(fine))
    placed = P(everything, None)
    return jax.shard_map(
        body,
        mesh=mesh,
        in_specs=(placed, placed),
        out_specs=(placed, placed, P(everything)),
        check_vma=False,
    )
```

```python
import jax
import jax.numpy as jnp
from jax import lax
from jax.sharding import Mesh, PartitionSpec as P

logit_scale = 100.0

fine = {"y": 4, "zl": 8, "zh": 4, "x": 4, "core": 2}
chip = ("x", "core")
blk = ("y", "zl")
ring = ((1, 1), (3, 2))
everything = ("y", "zl", "zh", "x", "core")


def axes(axis):
    return axis if isinstance(axis, tuple) else (axis,)


def gather(rows, axis):
    copies = jnp.broadcast_to(rows[None], (lax.axis_size(axis),) + rows.shape)
    return lax.all_to_all(copies, axis, 0, 0)


def swap(value, axis, step):
    return lax.ppermute(value, axis, [(i, i ^ step) for i in range(lax.axis_size(axis))])


def gather_by_swaps(rows, axis):
    me = lax.axis_index(axis)
    came = [rows] + [swap(rows, axis, p) for p in range(1, lax.axis_size(axis))]
    return jnp.stack([lax.select_n(me ^ k, *came) for k in range(len(came))])


def scatter_sum(parts, axis):
    return jnp.sum(
        lax.all_to_all(parts.astype(jnp.bfloat16), axis, 0, 0).astype(jnp.float32), axis=0
    )


def pieces(parts, axis):
    me = lax.axis_index(axis)
    return [lax.dynamic_index_in_dim(parts, me ^ p, 0, False) for p in range(parts.shape[0])]


def lse(values, dim):
    top = jnp.max(values, axis=dim, keepdims=True)
    return jnp.squeeze(top, dim) + jnp.log(jnp.sum(jnp.exp(values - top), axis=dim))


def gather_by_doubling(rows, axis, steps):
    for step, bit in steps:
        other = swap(rows, axis, step)
        upper = (lax.axis_index(axis) & bit) != 0
        rows = jnp.stack([jnp.where(upper, other, rows), jnp.where(upper, rows, other)])
    return rows


def scatter_sum_by_halving(parts, axis, steps):
    for step, bit in reversed(steps):
        upper = jnp.where((lax.axis_index(axis) & bit) != 0, 1, 0)
        given = lax.dynamic_index_in_dim(parts, 1 - upper, 0, False).astype(jnp.bfloat16)
        given = swap(given, axis, step).astype(jnp.float32)
        parts = lax.dynamic_index_in_dim(parts, upper, 0, False) + given
    return parts


def lse_over(row, col, row_axis, col_axis):
    n_row, n_col = lax.axis_size(row_axis), lax.axis_size(col_axis)
    here, there = lax.axis_index(col_axis), lax.axis_index(row_axis)
    same = (jnp.arange(n_col) == here)[:, None, None]
    sent = jnp.broadcast_to(jnp.where(same, row, col), (n_col, n_row, row.shape[0]))
    came = lax.all_to_all(sent.reshape(-1, row.shape[0]), axes(col_axis) + axes(row_axis), 0, 0)
    came = came.reshape(sent.shape)
    rows = lax.dynamic_index_in_dim(came, here, 0, False)
    cols = lax.dynamic_index_in_dim(came, there, 1, False)
    cols = jnp.where((jnp.arange(n_col) == here)[:, None], col, cols)
    return lse(rows, 0), lse(cols, 0)


def body(image_emb, text_emb):
    own_rows, width = image_emb.shape
    img_rows = gather(gather_by_doubling(image_emb, "zh", ring), chip)
    txt_cols = gather_by_swaps(gather(text_emb, "zl"), "y")
    img_rows = img_rows.reshape(img_rows.shape[0], -1, own_rows, width)
    row_lanes, col_lanes = img_rows.shape[:-1], txt_cols.shape[:-1]
    img_rows, txt_cols = img_rows.reshape(-1, width), txt_cols.reshape(-1, width)
    scores = logit_scale * jnp.dot(img_rows, txt_cols.T, preferred_element_type=jnp.float32)
    row_lse, col_lse = lse_over(lse(scores, 1), lse(scores, 0), chip, "y")
    row_lse, col_lse = lse_over(row_lse, col_lse, "zh", "zl")
    weights = (
        0.5 * (jnp.exp(scores - row_lse[:, None]) + jnp.exp(scores - col_lse[None, :]))
    ).astype(jnp.bfloat16)
    image_part = jnp.dot(weights, txt_cols, preferred_element_type=jnp.float32)
    image_part = image_part.reshape(row_lanes + (width,))
    text_part = lax.dot_general(
        weights, img_rows, (((0,), (0,)), ((), ())), preferred_element_type=jnp.float32
    )
    text_part = text_part.reshape(col_lanes + (width,))
    image_sum = scatter_sum(image_part, chip).reshape(2, 2, own_rows, width)
    own, near, opposite, other = pieces(text_part.astype(jnp.bfloat16), "y")
    came = [own, swap(opposite, "y", 2), swap(other, "y", 3)]
    image_sum, near = lax.optimization_barrier((image_sum, near))
    came.append(swap(near, "y", 1))
    text_sum = scatter_sum(sum(part.astype(jnp.float32) for part in came), "zl")
    image_sum = scatter_sum_by_halving(image_sum, "zh", ring)
    grad_image = logit_scale * image_sum - logit_scale * text_emb.astype(jnp.float32)
    grad_text = logit_scale * text_sum - logit_scale * image_emb.astype(jnp.float32)
    own_row = lax.axis_index(chip) * row_lanes[1] + lax.axis_index("zh")
    own_row_lse = lax.dynamic_slice_in_dim(row_lse, own_row * own_rows, own_rows, 0)
    own_col_lse = lax.dynamic_slice_in_dim(col_lse, lax.axis_index(blk) * own_rows, own_rows, 0)
    image_own, text_own = lax.optimization_barrier((image_emb, text_emb))
    diag = logit_scale * jnp.sum(
        image_own.astype(jnp.float32) * text_own.astype(jnp.float32), axis=1
    )
    row_loss = 0.5 * (own_row_lse + own_col_lse) - diag
    return (grad_image, grad_text, row_loss)


def solution(mesh):
    mesh = Mesh(mesh.devices.reshape(tuple(fine.values())), tuple(fine))
    placed = P(everything, None)
    return jax.shard_map(
        body,
        mesh=mesh,
        in_specs=(placed, placed),
        out_specs=(placed, placed, P(everything)),
        check_vma=False,
    )
```

```python
import jax
import jax.numpy as jnp
from jax import lax
from jax.sharding import Mesh, PartitionSpec as P

logit_scale = 100.0

fine = {"y": 4, "zl": 8, "zh": 4, "x": 4, "core": 2}
chip = ("x", "core")
blk = ("y", "zl")
ring = ((1, 1), (3, 2))
everything = ("y", "zl", "zh", "x", "core")


def axes(axis):
    return axis if isinstance(axis, tuple) else (axis,)


def gather(rows, axis):
    copies = jnp.broadcast_to(rows[None], (lax.axis_size(axis),) + rows.shape)
    return lax.all_to_all(copies, axis, 0, 0)


def swap(value, axis, step):
    return lax.ppermute(value, axis, [(i, i ^ step) for i in range(lax.axis_size(axis))])


def gather_by_swaps(rows, axis):
    me = lax.axis_index(axis)
    came = [rows] + [swap(rows, axis, p) for p in range(1, lax.axis_size(axis))]
    return jnp.stack([lax.select_n(me ^ k, *came) for k in range(len(came))])


def scatter_sum(parts, axis):
    return jnp.sum(
        lax.all_to_all(parts.astype(jnp.bfloat16), axis, 0, 0).astype(jnp.float32), axis=0
    )


def scatter_sum_by_swaps(parts, axis):
    me = lax.axis_index(axis)
    parts = parts.astype(jnp.bfloat16)
    own = [lax.dynamic_index_in_dim(parts, me ^ p, 0, False) for p in range(parts.shape[0])]
    came = own[:1] + [swap(own[p], axis, p) for p in range(1, parts.shape[0])]
    return sum(part.astype(jnp.float32) for part in came)


def lse(values, dim):
    top = jnp.max(values, axis=dim, keepdims=True)
    return jnp.squeeze(top, dim) + jnp.log(jnp.sum(jnp.exp(values - top), axis=dim))


def gather_by_doubling(rows, axis, steps):
    for step, bit in steps:
        other = swap(rows, axis, step)
        upper = (lax.axis_index(axis) & bit) != 0
        rows = jnp.stack([jnp.where(upper, other, rows), jnp.where(upper, rows, other)])
    return rows


def scatter_sum_by_halving(parts, axis, steps):
    for step, bit in reversed(steps):
        upper = jnp.where((lax.axis_index(axis) & bit) != 0, 1, 0)
        given = lax.dynamic_index_in_dim(parts, 1 - upper, 0, False).astype(jnp.bfloat16)
        given = swap(given, axis, step).astype(jnp.float32)
        parts = lax.dynamic_index_in_dim(parts, upper, 0, False) + given
    return parts


def lse_over(row, col, row_axis, col_axis):
    n_row, n_col = lax.axis_size(row_axis), lax.axis_size(col_axis)
    here, there = lax.axis_index(col_axis), lax.axis_index(row_axis)
    same = (jnp.arange(n_col) == here)[:, None, None]
    sent = jnp.broadcast_to(jnp.where(same, row, col), (n_col, n_row, row.shape[0]))
    came = lax.all_to_all(sent.reshape(-1, row.shape[0]), axes(col_axis) + axes(row_axis), 0, 0)
    came = came.reshape(sent.shape)
    rows = lax.dynamic_index_in_dim(came, here, 0, False)
    cols = lax.dynamic_index_in_dim(came, there, 1, False)
    cols = jnp.where((jnp.arange(n_col) == here)[:, None], col, cols)
    return lse(rows, 0), lse(cols, 0)


def body(image_emb, text_emb):
    own_rows, width = image_emb.shape
    img_rows = gather(gather_by_doubling(image_emb, "zh", ring), chip)
    txt_cols = gather_by_swaps(gather(text_emb, "zl"), "y")
    img_rows = img_rows.reshape(img_rows.shape[0], -1, own_rows, width)
    row_lanes, col_lanes = img_rows.shape[:-1], txt_cols.shape[:-1]
    img_rows, txt_cols = img_rows.reshape(-1, width), txt_cols.reshape(-1, width)
    scores = logit_scale * jnp.dot(img_rows, txt_cols.T, preferred_element_type=jnp.float32)
    row_lse, col_lse = lse_over(lse(scores, 1), lse(scores, 0), chip, "y")
    row_lse, col_lse = lse_over(row_lse, col_lse, "zh", "zl")
    weights = (
        0.5 * (jnp.exp(scores - row_lse[:, None]) + jnp.exp(scores - col_lse[None, :]))
    ).astype(jnp.bfloat16)
    image_part = jnp.dot(weights, txt_cols, preferred_element_type=jnp.float32)
    image_part = image_part.reshape(row_lanes + (width,))
    turned = logit_scale * jnp.dot(txt_cols, img_rows.T, preferred_element_type=jnp.float32)
    turned = (
        0.5 * (jnp.exp(turned - row_lse[None, :]) + jnp.exp(turned - col_lse[:, None]))
    ).astype(jnp.bfloat16)
    text_part = jnp.dot(turned, img_rows, preferred_element_type=jnp.float32)
    text_part = text_part.reshape(col_lanes + (width,))
    image_sum = scatter_sum(image_part, chip).reshape(2, 2, own_rows, width)
    image_sum = scatter_sum_by_halving(image_sum, "zh", ring)
    text_sum = scatter_sum(scatter_sum_by_swaps(text_part, "y"), "zl")
    grad_image = logit_scale * image_sum - logit_scale * text_emb.astype(jnp.float32)
    grad_text = logit_scale * text_sum - logit_scale * image_emb.astype(jnp.float32)
    own_row = lax.axis_index(chip) * row_lanes[1] + lax.axis_index("zh")
    own_row_lse = lax.dynamic_slice_in_dim(row_lse, own_row * own_rows, own_rows, 0)
    own_col_lse = lax.dynamic_slice_in_dim(col_lse, lax.axis_index(blk) * own_rows, own_rows, 0)
    image_own, text_own = lax.optimization_barrier((image_emb, text_emb))
    diag = logit_scale * jnp.sum(
        image_own.astype(jnp.float32) * text_own.astype(jnp.float32), axis=1
    )
    row_loss = 0.5 * (own_row_lse + own_col_lse) - diag
    return (grad_image, grad_text, row_loss)


def solution(mesh):
    mesh = Mesh(mesh.devices.reshape(tuple(fine.values())), tuple(fine))
    placed = P(everything, None)
    return jax.shard_map(
        body,
        mesh=mesh,
        in_specs=(placed, placed),
        out_specs=(placed, placed, P(everything)),
        check_vma=False,
    )
```
